512 devices in a mesh: lo: 16 (over y, x), hi: 32 (over z, core).
Axes of the slice: x: 4, y: 4, z: 16, core: 2. Of those that a mesh axis runs over, the one named last changes fastest.
Arguments:
- points: bfloat16 [32, 16, 64, 4096], P('hi', 'lo'), may hold values from -6 to 6
- rhs: bfloat16 [32, 16, 4096, 128], P('hi', 'lo'), may hold values from -6 to 6
- order: int32 [32, 16, 4096], P('hi', 'lo'), may hold values from 0 to 4095, each once within a row
- anchors: bfloat16 [32, 16, 11, 64, 128], P('hi', 'lo'), may hold values from -6 to 6
- coupling: float32 [32, 16, 11, 128, 128], P('hi', 'lo'), may hold values from -18 to 18
Outputs:
- product: float32 [32, 16, 4096, 128], P('hi', 'lo')
The draws below stay inside these ranges and needn't reach their ends.
All inputs are finite; a program needn't handle non-finite values.
Results may differ from the reference program's by a relative error of at most 0.0041.
Values sent between devices are 32-bit elements; how exact they have to be, the bound alone decides.
A program may use at most 128 MiB of HBM per device.

```python
import math
import jax
import jax.numpy as jnp
from jax import lax

W = 64
R = 128
NRHS = 128
PTS_DEV = 4096
HIGH = 32
LOW = 16
SETS = 11


def block_levels(rng, shape, cuts, smallest, high):
    factor_of = 1.0
    for position, shards_of in cuts:
        steps = jax.random.uniform(jax.random.fold_in(jax.random.fold_in(rng, 6), position), (shards_of,), jnp.float32, smallest / len(cuts), high / len(cuts))
        factor_of = factor_of * jnp.repeat(jnp.exp(steps), shape[position] // shards_of).reshape((-1,) + (1,) * (len(shape) - 1 - position))
    return factor_of


def bell_draw(stream_key, extent, scale, limit, pieces=(), held_as=jnp.bfloat16):
    level = block_levels(stream_key, extent, pieces, -0.22, 0.18) if pieces else 1.0
    values = jax.random.normal(stream_key, extent, jnp.float32) * scale * level
    return jnp.minimum(jnp.maximum(values, -limit), limit).astype(held_as)


def setup_inputs(seed: int = 0) -> dict:
    keys = jax.random.split(jax.random.key(seed), 6)
    return {
        "points": bell_draw(keys[0], (HIGH, LOW, W, PTS_DEV), 1.0, 6.0, ((0, 32), (1, 16))),
        "rhs": bell_draw(keys[1], (HIGH, LOW, PTS_DEV, NRHS), 1.0, 6.0, ((0, 32), (1, 16))),
        "order": jax.vmap(lambda own: jax.random.permutation(own, PTS_DEV))(jax.random.split(keys[2], HIGH * LOW)).reshape((HIGH, LOW, PTS_DEV)).astype(jnp.int32),
        "anchors": bell_draw(keys[3], (HIGH, LOW, SETS, W, R), 1.0, 6.0, ((0, 32), (1, 16))),
        "coupling": bell_draw(keys[4], (HIGH, LOW, SETS, R, R), 3.0, 18.0, ((0, 32), (1, 16)), jnp.float32),
    }


def kernel(left_pts, right_pts):
    cross_dot = lax.dot_general(left_pts, right_pts, (((0,), (0,)), ((), ())), preferred_element_type=jnp.float32)
    left_wide = left_pts.astype(jnp.float32)
    right_wide = right_pts.astype(jnp.float32)
    sq_dist = lax.optimization_barrier(jnp.sum(left_wide * left_wide, 0))[:, None] + lax.optimization_barrier(jnp.sum(right_wide * right_wide, 0))[None, :] - 2.0 * cross_dot
    return jnp.exp(sq_dist * (-2.0 / left_pts.shape[0]))

def far_basis(leaf_pts, anchor_set):
    emb_width = anchor_set.shape[1]
    far_sets = anchor_set.shape[0] - 2
    flat_anchors = jnp.transpose(anchor_set[2:], (1, 0, 2)).reshape(emb_width, far_sets * anchor_set.shape[2])
    return kernel(leaf_pts, flat_anchors).astype(jnp.bfloat16)

def contract_rows(basis_block, row_block):
    return lax.dot_general(basis_block, row_block, (((0,), (0,)), ((), ())), preferred_element_type=jnp.float32)

def apply_device(leaf_pts, leaf_rows, anchor_set, core_set, sibling_coef, perm_rows, basis_far):
    pts_count = leaf_pts.shape[1]
    leaf_size = pts_count // 2
    far_sets = anchor_set.shape[0] - 2
    rank_size = anchor_set.shape[2]
    rhs_count = leaf_rows.shape[1]
    level_scale = jnp.array([1.0 / math.sqrt(pts_count * 2.0 ** level) for level in range(far_sets)], jnp.float32)
    scaled = sibling_coef * level_scale[:, None, None]
    far_mix = jnp.einsum('lrs,lsn->lrn', core_set[2:], scaled, precision=lax.Precision.HIGHEST)
    far_mix = far_mix.astype(jnp.bfloat16).reshape(far_sets * rank_size, rhs_count)
    leaf_parts = []
    leaf_bases = []
    leaf_coefs = []
    for leaf_half in range(2):
        block_pts = leaf_pts[:, leaf_half * leaf_size:(leaf_half + 1) * leaf_size]
        block_rows = leaf_rows[leaf_half * leaf_size:(leaf_half + 1) * leaf_size]
        dense_block = kernel(block_pts, block_pts).astype(jnp.bfloat16)
        leaf_parts.append(jnp.dot(dense_block, block_rows, preferred_element_type=jnp.float32))
        basis_block = kernel(block_pts, anchor_set[leaf_half]).astype(jnp.bfloat16)
        leaf_bases.append(basis_block)
        leaf_coefs.append(contract_rows(basis_block, block_rows))
    local_scale = 1.0 / math.sqrt(leaf_size)
    for leaf_half in range(2):
        mixed_coef = jnp.dot(core_set[leaf_half], leaf_coefs[1 - leaf_half] * local_scale, precision=lax.Precision.HIGHEST)
        mixed_coef = mixed_coef.astype(jnp.bfloat16)
        leaf_parts[leaf_half] = leaf_parts[leaf_half] + jnp.dot(leaf_bases[leaf_half], mixed_coef, preferred_element_type=jnp.float32)
    result = jnp.concatenate(leaf_parts, 0) + jnp.dot(basis_far, far_mix, preferred_element_type=jnp.float32)
    return jnp.zeros_like(result).at[perm_rows].set(result)

def reference(points, rhs, order, anchors, coupling):
    dev_count = HIGH * LOW
    far_sets = SETS - 2
    all_pts = points.reshape(dev_count, W, PTS_DEV)
    all_rows = rhs.reshape(dev_count, PTS_DEV, NRHS)
    all_order = order.reshape(dev_count, PTS_DEV)
    all_anchors = anchors.reshape(dev_count, SETS, W, R)
    all_cores = coupling.reshape(dev_count, SETS, R, R)

    def partial_of(items):
        pts_one, rows_one, order_one, anchor_one = items
        leaf_pts = pts_one[:, order_one]
        leaf_rows = rows_one[order_one]
        return contract_rows(far_basis(leaf_pts, anchor_one), leaf_rows).reshape(far_sets, R, NRHS)
    partials = lax.map(partial_of, (all_pts, all_rows, all_order, all_anchors))
    siblings = []
    for level in range(far_sets):
        width_now = 2 ** level
        groups = lax.optimization_barrier(jnp.sum(partials[:, level].reshape(dev_count // width_now, width_now, R, NRHS), axis=1))
        swapped = groups.reshape(dev_count // (2 * width_now), 2, R, NRHS)[:, ::-1].reshape(dev_count // width_now, R, NRHS)
        siblings.append(jnp.repeat(swapped, width_now, axis=0))
    sibling_all = jnp.stack(siblings, 1)

    def apply_one(items):
        pts_one, rows_one, order_one, anchor_one, core_one, sib_one = items
        leaf_pts = pts_one[:, order_one]
        leaf_rows = rows_one[order_one]
        basis_far = far_basis(leaf_pts, anchor_one)
        return apply_device(leaf_pts, leaf_rows, anchor_one, core_one, sib_one, order_one, basis_far)
    result = lax.map(apply_one, (all_pts, all_rows, all_order, all_anchors, all_cores, sibling_all))
    return result.reshape(HIGH, LOW, PTS_DEV, NRHS)
```

```python
import functools
import math

import jax
import jax.numpy as jnp
from jax import lax
from jax.experimental import pallas as pl
from jax.experimental.pallas import tpu as pltpu
from jax.sharding import PartitionSpec as P

bf16 = jnp.bfloat16
f32 = jnp.float32
MESH = pl.DeviceIdType.MESH

WIDTH = 64
RANK = 128
RHS = 128
PTS = 4096
LEAF = 2048
SIDE = 4
LO = 16
UP = 5
DOWN = 4
UPW, DOWNW = UP * RANK, DOWN * RANK
FARW = UPW + DOWNW
ALLW = FARW + 2 * RANK
ROWS = RHS // LO
DEPTH = 128
EXPONENT = math.log2(math.e) * 4.0 / WIDTH
SIGN = 32.0
COLS = 1024


def dot(a, b):
    return jnp.dot(a, b, preferred_element_type=f32)


def dot_nt(a, b, **kw):
    return lax.dot_general(a, b, (((1,), (1,)), ((), ())), preferred_element_type=f32, **kw)


def gauss(a, b):
    return jnp.exp2(dot(a, b) * EXPONENT).astype(bf16)


def flip(index, mask):
    for bit in range(5):
        if mask >> bit & 1:
            step = 1 << bit
            index = index + step * (1 - 2 * (index // step % 2))
    return index


def split3(value):
    first = value.astype(bf16).astype(f32)
    rest = value - first
    second = rest.astype(bf16).astype(f32)
    return first, second, rest - second


def extended(cols, sign, offset, mirrored):
    n = cols.shape[1]
    half = -0.5 * jnp.sum(cols * cols, axis=0, keepdims=True)
    first, second, third = split3(half)
    row = lax.broadcasted_iota(jnp.int32, (16, n), 0)
    base = 3 if mirrored else 0
    block = jnp.where((row < 6), 1.0, 0.0)
    block = jnp.where(row == base, first, block)
    block = jnp.where(row == base + 1, second, block)
    block = jnp.where(row == base + 2, third, block)
    block = jnp.where(row == 6, sign, block)
    return jnp.where(row == 7, offset, block)


def body(
    points, rhs, order, anchors, coupling, out,
    xr, xlt, zlt, xt, vt, yt, tt, srow,
    pt_up, pt_down, et, rs_up, rs_down, q_up, a_in, g_up, b_in, ct_up, ct_down, ag_down,
    su_s, su_r, sd_s, sd_r, gu_s, gu_r, gd_s, gd_r, a_s, a_r, b_s, b_r,
):
    lo, hi = lax.axis_index("lo"), lax.axis_index("hi")
    y, x = lo // SIDE, lo % SIDE
    mine = pl.ds(pl.multiple_of(ROWS * lo, ROWS), ROWS)

    def at(d):
        dy, dx = d // SIDE, d % SIDE
        onward = (y + dy) % SIDE * SIDE + (x + dx) % SIDE
        back = (y + SIDE - dy) % SIDE * SIDE + (x + SIDE - dx) % SIDE
        return onward, back

    def rows_of(index):
        return pl.ds(pl.multiple_of(ROWS * index, ROWS), ROWS)

    def copy(src, dst, send, recv, where):
        return pltpu.make_async_remote_copy(
            src_ref=src, dst_ref=dst, send_sem=send, recv_sem=recv, device_id=where, device_id_type=MESH
        )

    def scatter(d, src, dst, send, recv):
        onward, _ = at(d)
        return copy(src.at[rows_of(onward)], dst.at[lo], send.at[d], recv.at[d], {"lo": onward, "hi": hi})

    def gather_up(d):
        onward, _ = at(d)
        return copy(ct_up.at[mine], ct_up.at[mine], gu_s.at[d], gu_r.at[d], {"lo": onward, "hi": hi})

    def gather_down(d):
        onward, _ = at(d)
        return copy(ag_down.at[onward], ct_down.at[mine], gd_s.at[d], gd_r.at[d], {"lo": onward, "hi": hi})

    def across_near(m):
        return copy(q_up, a_in.at[m - 1], a_s.at[m - 1], a_r.at[m - 1], {"lo": lo, "hi": flip(hi, m)})

    def across_far(m):
        level = 0 if m == 1 else 1 if m < 4 else 2
        src = g_up.at[:, level * RANK : (level + 1) * RANK]
        return copy(src, b_in.at[m - 1], b_s.at[m - 1], b_r.at[m - 1], {"lo": lo, "hi": flip(hi, 4 * m)})

    def each(fn):
        def step(d, c):
            fn(d)
            return c

        lax.fori_loop(1, LO, step, 0)

    barrier = pltpu.get_barrier_semaphore()
    each(lambda d: pl.semaphore_signal(barrier, inc=1, device_id={"lo": at(d)[0], "hi": hi}, device_id_type=MESH))
    partners = [m for m in range(1, 4)] + [4 * m for m in range(1, 8)]
    for m in partners:
        pl.semaphore_signal(barrier, inc=1, device_id={"lo": lo, "hi": flip(hi, m)}, device_id_type=MESH)

    lane_hot, row_hot = [], []
    for k in range(LEAF // 128, PTS // 128):
        line = order[k : k + 1, :]
        lane_hot.append(jnp.where(lax.broadcasted_iota(jnp.int32, (128, 128), 0) == (line & 127), 1.0, 0.0).astype(bf16))
        row_hot.append(jnp.where(lax.broadcasted_iota(jnp.int32, (32, 128), 0) == (line >> 7), 1.0, 0.0).astype(bf16))
    in_second = dot_nt(jnp.concatenate(row_hot, 1), jnp.concatenate(lane_hot, 1))
    signs = (2.0 * in_second - 1.0) * SIGN
    for k in range(PTS // 128):
        srow[:, k * 128 : (k + 1) * 128] = signs[k : k + 1, :]

    for c in range(0, PTS, COLS):
        cut = slice(c, c + COLS)
        cols = points[:, cut].astype(f32)
        xr[0:WIDTH, cut] = points[:, cut]
        xr[WIDTH : WIDTH + 16, cut] = extended(cols, srow[:, cut], 1.0, False).astype(bf16)
        xr[WIDTH + 16 : DEPTH, cut] = jnp.zeros((DEPTH - WIDTH - 16, COLS), bf16)
        left = jnp.concatenate(
            [cols, extended(cols, srow[:, cut], -SIGN * SIGN, True), jnp.zeros((DEPTH - WIDTH - 16, COLS), f32)], 0
        )
        xlt[cut, :] = left.T.astype(bf16)
        xt[:, cut] = rhs[cut, :].astype(f32).T.astype(bf16)
    sets = [2 + DOWN + j for j in range(UP)] + [2 + j for j in range(DOWN)] + [0, 1]
    for k, s in enumerate(sets):
        cols = anchors[s].astype(f32)
        sign = SIGN * (2 * s - 1) if s < 2 else 0.0
        offset = -SIGN * SIGN if s < 2 else 0.0
        left = jnp.concatenate(
            [cols, extended(cols, sign, offset, True), jnp.zeros((DEPTH - WIDTH - 16, RANK), f32)], 0
        )
        zlt[k * RANK : (k + 1) * RANK, :] = left.T.astype(bf16)

    def basis(first, width, total):
        total[...] = jnp.zeros_like(total)

        def step(i, c):
            cut = pl.ds(pl.multiple_of(i * LEAF, LEAF), LEAF)
            tile = gauss(zlt[first : first + width], xr[:, cut])
            vt[first : first + width, cut] = tile
            total[...] += dot_nt(xt[:, cut], tile)
            return c

        lax.fori_loop(0, PTS // LEAF, step, 0)

    basis(0, UPW, pt_up)
    pl.semaphore_wait(barrier, LO - 1 + len(partners))
    each(lambda d: scatter(d, pt_up, rs_up, su_s, su_r).start())
    rs_up[lo] = pt_up[mine, :]
    basis(UPW, DOWNW, pt_down)
    each(lambda d: scatter(d, pt_down, rs_down, sd_s, sd_r).start())
    rs_down[lo] = pt_down[mine, :]
    basis(FARW, 2 * RANK, et)

    def mix(coef, core, scale):
        return dot_nt(coef * scale, core, precision=lax.Precision.HIGHEST).astype(bf16)

    for a in range(2):
        coef = et[:, (1 - a) * RANK : (2 - a) * RANK]
        tt[:, FARW + a * RANK : FARW + (a + 1) * RANK] = mix(coef, coupling[a], 1.0 / math.sqrt(LEAF))

    def near_sums():
        each(lambda d: scatter(d, pt_up, rs_up, su_s, su_r).wait_recv())
        total = rs_up[0]
        for g in range(1, LO):
            total = total + rs_up[g]
        q_up[...] = total
        for m in range(1, 4):
            across_near(m).start()

    def far_sums():
        for m in range(1, 4):
            across_near(m).wait_recv()
        lanes = slice(2 * RANK, UPW)
        g_up[...] = (q_up[:, lanes] + a_in[0, :, lanes]) + (a_in[1, :, lanes] + a_in[2, :, lanes])
        for m in range(1, 8):
            across_far(m).start()
        ct_up[mine, 0:RANK] = a_in[0, :, 0:RANK]
        ct_up[mine, RANK : 2 * RANK] = a_in[1, :, RANK : 2 * RANK] + a_in[2, :, RANK : 2 * RANK]

    def send_down():
        each(lambda d: scatter(d, pt_down, rs_down, sd_s, sd_r).wait_recv())
        for j in range(DOWN):
            lanes = slice(j * RANK, (j + 1) * RANK)
            sums = [rs_down[g, :, lanes] for g in range(LO)]
            for _ in range(j):
                sums = [sums[2 * k] + sums[2 * k + 1] for k in range(len(sums) // 2)]
            for g in range(LO):
                ag_down[g, :, lanes] = sums[(g >> j) ^ 1]
        each(lambda d: gather_down(d).start())
        ct_down[mine, :] = ag_down[lo]

    def send_up():
        for m in range(1, 8):
            across_far(m).wait_recv()
        ct_up[mine, 2 * RANK : 3 * RANK] = b_in[0]
        ct_up[mine, 3 * RANK : 4 * RANK] = b_in[1] + b_in[2]
        ct_up[mine, 4 * RANK : 5 * RANK] = (b_in[3] + b_in[4]) + (b_in[5] + b_in[6])
        each(lambda d: gather_up(d).start())

    def dense(i, c):
        cut = pl.ds(pl.multiple_of(i * COLS, COLS), COLS)
        right = xr[:, cut]
        total = dot(tt[:, FARW:ALLW], vt[FARW:ALLW, cut])
        for r in range(0, PTS, COLS):
            total = total + dot(xt[:, r : r + COLS], gauss(xlt[r : r + COLS, :], right))
        yt[:, cut] = total

        @pl.when(i == 0)
        def _():
            near_sums()

        @pl.when(i == 1)
        def _():
            far_sums()
            send_down()

        @pl.when(i == 2)
        def _():
            send_up()

        return c

    lax.fori_loop(0, PTS // COLS, dense, 0)

    each(lambda d: gather_down(d).wait_recv())
    for j in range(DOWN):
        scale = 1.0 / math.sqrt(PTS * 2.0**j)
        lanes = slice(j * RANK, (j + 1) * RANK)
        tt[:, UPW + j * RANK : UPW + (j + 1) * RANK] = mix(ct_down[:, lanes], coupling[2 + j], scale)
    each(lambda d: gather_up(d).wait_recv())
    for j in range(UP):
        scale = 1.0 / math.sqrt(PTS * 2.0 ** (DOWN + j))
        lanes = slice(j * RANK, (j + 1) * RANK)
        tt[:, lanes] = mix(ct_up[:, lanes], coupling[2 + DOWN + j], scale)
    for c in range(0, PTS, COLS):
        cut = slice(c, c + COLS)
        out[cut, :] = (yt[:, cut] + dot(tt[:, 0:FARW], vt[0:FARW, cut])).T

    each(lambda d: scatter(d, pt_up, rs_up, su_s, su_r).wait_send())
    each(lambda d: scatter(d, pt_down, rs_down, sd_s, sd_r).wait_send())
    each(lambda d: gather_up(d).wait_send())
    each(lambda d: gather_down(d).wait_send())
    for m in range(1, 4):
        across_near(m).wait_send()
    for m in range(1, 8):
        across_far(m).wait_send()


def per_device(points, rhs, order, anchors, coupling):
    vmem = pl.BlockSpec(memory_space=pltpu.VMEM)
    scratch = [
        ((DEPTH, PTS), bf16),
        ((PTS, DEPTH), bf16),
        ((ALLW, DEPTH), bf16),
        ((RHS, PTS), bf16),
        ((ALLW, PTS), bf16),
        ((RHS, PTS), f32),
        ((RHS, ALLW), bf16),
        ((1, PTS), f32),
        ((RHS, UPW), f32),
        ((RHS, DOWNW), f32),
        ((RHS, 2 * RANK), f32),
        ((LO, ROWS, UPW), f32),
        ((LO, ROWS, DOWNW), f32),
        ((ROWS, UPW), f32),
        ((3, ROWS, UPW), f32),
        ((ROWS, 3 * RANK), f32),
        ((7, ROWS, RANK), f32),
        ((RHS, UPW), f32),
        ((RHS, DOWNW), f32),
        ((LO, ROWS, DOWNW), f32),
    ]
    sems = [pltpu.SemaphoreType.DMA((LO,))] * 8 + [pltpu.SemaphoreType.DMA((3,))] * 2 + [pltpu.SemaphoreType.DMA((7,))] * 2
    out = pl.pallas_call(
        body,
        out_shape=jax.ShapeDtypeStruct((PTS, RHS), f32),
        in_specs=[vmem] * 5,
        out_specs=vmem,
        scratch_shapes=[pltpu.VMEM(s, d) for s, d in scratch] + sems,
        compiler_params=pltpu.CompilerParams(
            collective_id=0, has_side_effects=True, vmem_limit_bytes=56 * 2**20
        ),
        name="hodlr",
    )(points[0, 0], rhs[0, 0], order[0, 0].reshape(PTS // 128, 128), anchors[0, 0], coupling[0, 0])
    return out[None, None]


def solution(mesh):
    return jax.shard_map(
        per_device,
        mesh=mesh,
        in_specs=(
            P("hi", "lo", None, None),
            P("hi", "lo", None, None),
            P("hi", "lo", None),
            P("hi", "lo", None, None, None),
            P("hi", "lo", None, None, None),
        ),
        out_specs=P("hi", "lo", None, None),
        check_vma=False,
    )
```

```python
import math

import jax
import jax.numpy as jnp
from jax import lax
from jax.experimental import pallas as pl
from jax.experimental.pallas import tpu as pltpu
from jax.sharding import PartitionSpec as P

bf16 = jnp.bfloat16
f32 = jnp.float32
MESH = pl.DeviceIdType.MESH

WIDTH = 64
RANK = 128
RHS = 128
PTS = 4096
LEAF = 2048
SIDE = 4
LO = 16
FIRST = 6
TOP, LOW = 3, 6
INSIDE = 4
TOPW, LOWW = TOP * RANK, LOW * RANK
FARW = TOPW + LOWW
ALLW = FARW + 2 * RANK
ROWS = RHS // LO
DEPTH = 128
EXPONENT = math.log2(math.e) * 4.0 / WIDTH
SIGN = 32.0
COLS = 1024
STEP = 512
SEND_NEAR, SEND_LOW, SEND_TOP = 0, 1, 5


def dot(a, b):
    return jnp.dot(a, b, preferred_element_type=f32)


def dot_nt(a, b, **kw):
    return lax.dot_general(a, b, (((1,), (1,)), ((), ())), preferred_element_type=f32, **kw)


def gauss(a, b):
    return jnp.exp2(dot(a, b) * EXPONENT).astype(bf16)


def flip(index, mask):
    for bit in range(5):
        if mask >> bit & 1:
            step = 1 << bit
            index = index + step * (1 - 2 * (index // step % 2))
    return index


def split3(value):
    first = value.astype(bf16).astype(f32)
    rest = value - first
    second = rest.astype(bf16).astype(f32)
    return first, second, rest - second


def extended(cols, sign, offset, mirrored):
    n = cols.shape[1]
    half = -0.5 * jnp.sum(cols * cols, axis=0, keepdims=True)
    first, second, third = split3(half)
    row = lax.broadcasted_iota(jnp.int32, (16, n), 0)
    base = 3 if mirrored else 0
    block = jnp.where((row < 6), 1.0, 0.0)
    block = jnp.where(row == base, first, block)
    block = jnp.where(row == base + 1, second, block)
    block = jnp.where(row == base + 2, third, block)
    block = jnp.where(row == 6, sign, block)
    return jnp.where(row == 7, offset, block)


def body(
    points_in, rhs_in, order_in, anchors_in, coupling_in, out,
    points, rhs, order, anchors, coupling,
    xr, xlt, zlt, xt, vt, yt, tt, srow,
    pt_top, pt_low, et, rs_top, rs_low, q_top, q_low, a_in, e_in, g_top, b_in, ct_top, ct_low, ag_low,
    in_s, su_s, su_r, sd_s, sd_r, gu_s, gu_r, gd_s, gd_r, a_s, a_r, e_s, e_r, b_s, b_r,
):
    arriving = [
        pltpu.make_async_copy(src, dst, in_s.at[k])
        for k, (src, dst) in enumerate(
            ((points_in, points), (anchors_in, anchors), (rhs_in, rhs), (order_in, order), (coupling_in, coupling))
        )
    ]
    for piece in arriving:
        piece.start()

    lo, hi = lax.axis_index("lo"), lax.axis_index("hi")
    y, x = lo // SIDE, lo % SIDE
    mine = pl.ds(pl.multiple_of(ROWS * lo, ROWS), ROWS)

    def onward(d):
        return (y + d // SIDE) % SIDE * SIDE + (x + d % SIDE) % SIDE

    def rows_of(index):
        return pl.ds(pl.multiple_of(ROWS * index, ROWS), ROWS)

    def copy(src, dst, send, recv, where):
        return pltpu.make_async_remote_copy(
            src_ref=src, dst_ref=dst, send_sem=send, recv_sem=recv, device_id=where, device_id_type=MESH
        )

    def scatter(d, src, dst, send, recv):
        there = onward(d)
        return copy(src.at[rows_of(there)], dst.at[lo], send.at[d], recv.at[d], {"lo": there, "hi": hi})

    def scatter_top(d):
        return scatter(d, pt_top, rs_top, su_s, su_r)

    def scatter_low(d):
        return scatter(d, pt_low, rs_low, sd_s, sd_r)

    def gather_top(d):
        return copy(ct_top.at[mine], ct_top.at[mine], gu_s.at[d], gu_r.at[d], {"lo": onward(d), "hi": hi})

    def gather_low(d):
        there = onward(d)
        return copy(ag_low.at[there], ct_low.at[mine], gd_s.at[d], gd_r.at[d], {"lo": there, "hi": hi})

    def near_top(m):
        return copy(q_top, a_in.at[m - 1], a_s.at[m - 1], a_r.at[m - 1], {"lo": lo, "hi": flip(hi, m)})

    def near_low(m):
        src = q_low.at[:, 0:RANK] if m == 1 else q_low.at[:, RANK : 2 * RANK]
        return copy(src, e_in.at[m - 1], e_s.at[m - 1], e_r.at[m - 1], {"lo": lo, "hi": flip(hi, m)})

    def far_top(m):
        level = 0 if m == 1 else 1 if m < 4 else 2
        src = g_top.at[:, level * RANK : (level + 1) * RANK]
        return copy(src, b_in.at[m - 1], b_s.at[m - 1], b_r.at[m - 1], {"lo": lo, "hi": flip(hi, 4 * m)})

    def each(fn):
        def step(d, c):
            fn(d)
            return c

        lax.fori_loop(1, LO, step, 0)

    barrier = pltpu.get_barrier_semaphore()
    each(lambda d: pl.semaphore_signal(barrier, inc=1, device_id={"lo": onward(d), "hi": hi}, device_id_type=MESH))
    partners = [m for m in range(1, 4)] + [4 * m for m in range(1, 8)]
    for m in partners:
        pl.semaphore_signal(barrier, inc=1, device_id={"lo": lo, "hi": flip(hi, m)}, device_id_type=MESH)

    pad = DEPTH - WIDTH - 16
    arriving[0].wait()
    for c in range(0, PTS, COLS):
        cut = slice(c, c + COLS)
        xr[0:WIDTH, cut] = points[:, cut]
        xr[WIDTH : WIDTH + 16, cut] = extended(points[:, cut].astype(f32), 0.0, 1.0, False).astype(bf16)
        xr[WIDTH + 16 : DEPTH, cut] = jnp.zeros((pad, COLS), bf16)

    sets = [2 + FIRST + j for j in range(TOP)] + [2 + j for j in range(LOW)] + [0, 1]

    def anchor_rows(first, last):
        for k in range(first, last):
            s = sets[k]
            cols = anchors[s].astype(f32)
            sign = SIGN * (2 * s - 1) if s < 2 else 0.0
            offset = -SIGN * SIGN if s < 2 else 0.0
            left = jnp.concatenate([cols, extended(cols, sign, offset, True), jnp.zeros((pad, RANK), f32)], 0)
            zlt[k * RANK : (k + 1) * RANK, :] = left.T.astype(bf16)

    arriving[1].wait()
    anchor_rows(0, TOP)
    arriving[2].wait()
    for c in range(0, PTS, COLS):
        cut = slice(c, c + COLS)
        xt[:, cut] = rhs[cut, :].T

    def basis(first, width, piece, sums):
        total = None
        for c in range(0, PTS, piece):
            cut = slice(c, c + piece)
            tile = gauss(zlt[first : first + width], xr[:, cut])
            vt[first : first + width, cut] = tile
            part = dot_nt(xt[:, cut], tile)
            total = part if total is None else total + part
        sums[...] = total

    basis(0, TOPW, 1024, pt_top)
    pl.semaphore_wait(barrier, LO - 1 + len(partners))
    each(lambda d: scatter_top(d).start())
    rs_top[lo] = pt_top[mine, :]
    anchor_rows(TOP, TOP + LOW)
    basis(TOPW, LOWW, 1024, pt_low)
    each(lambda d: scatter_low(d).start())
    rs_low[lo] = pt_low[mine, :]

    each(lambda d: scatter_top(d).wait_recv())
    total = rs_top[0]
    for g in range(1, LO):
        total = total + rs_top[g]
    q_top[...] = total
    for m in range(1, 4):
        near_top(m).start()

    arriving[3].wait()
    lane_hot, row_hot = [], []
    for k in range(LEAF // 128, PTS // 128):
        line = order[k : k + 1, :]
        lane_hot.append(jnp.where(lax.broadcasted_iota(jnp.int32, (128, 128), 0) == (line & 127), 1.0, 0.0).astype(bf16))
        row_hot.append(jnp.where(lax.broadcasted_iota(jnp.int32, (32, 128), 0) == (line >> 7), 1.0, 0.0).astype(bf16))
    in_second = dot_nt(jnp.concatenate(row_hot, 1), jnp.concatenate(lane_hot, 1))
    signs = (2.0 * in_second - 1.0) * SIGN
    for k in range(PTS // 128):
        srow[:, k * 128 : (k + 1) * 128] = signs[k : k + 1, :]
    for c in range(0, PTS, COLS):
        cut = slice(c, c + COLS)
        cols = points[:, cut].astype(f32)
        xr[WIDTH : WIDTH + 16, cut] = extended(cols, srow[:, cut], 1.0, False).astype(bf16)
        left = jnp.concatenate([cols, extended(cols, srow[:, cut], -SIGN * SIGN, True), jnp.zeros((pad, COLS), f32)], 0)
        xlt[cut, :] = left.T.astype(bf16)
    anchor_rows(TOP + LOW, TOP + LOW + 2)

    for m in range(1, 4):
        near_top(m).wait_recv()
    g_top[...] = (q_top[...] + a_in[0]) + (a_in[1] + a_in[2])
    for m in range(1, 8):
        far_top(m).start()

    basis(FARW, 2 * RANK, 2048, et)
    arriving[4].wait()

    def mix(coef, core, scale):
        return dot_nt(coef * scale, core, precision=lax.Precision.HIGHEST).astype(bf16)

    for a in range(2):
        coef = et[:, (1 - a) * RANK : (2 - a) * RANK]
        tt[:, FARW + a * RANK : FARW + (a + 1) * RANK] = mix(coef, coupling[a], 1.0 / math.sqrt(LEAF))

    def send_near():
        each(lambda d: scatter_low(d).wait_recv())
        lanes = slice(INSIDE * RANK, LOWW)
        total = rs_low[0, :, lanes]
        for g in range(1, LO):
            total = total + rs_low[g, :, lanes]
        q_low[...] = total
        for m in range(1, 4):
            near_low(m).start()
        for j in range(INSIDE):
            lanes = slice(j * RANK, (j + 1) * RANK)
            sums = [rs_low[g, :, lanes] for g in range(LO)]
            for _ in range(j):
                sums = [sums[2 * k] + sums[2 * k + 1] for k in range(len(sums) // 2)]
            for g in range(LO):
                ag_low[g, :, lanes] = sums[(g >> j) ^ 1]

    def send_low():
        for m in range(1, 4):
            near_low(m).wait_recv()
        fourth, fifth = e_in[0], e_in[1] + e_in[2]
        for g in range(LO):
            ag_low[g, :, INSIDE * RANK : (INSIDE + 1) * RANK] = fourth
            ag_low[g, :, (INSIDE + 1) * RANK : LOWW] = fifth
        each(lambda d: gather_low(d).start())
        ct_low[mine, :] = ag_low[lo]

    def send_top():
        for m in range(1, 8):
            far_top(m).wait_recv()
        ct_top[mine, 0:RANK] = b_in[0]
        ct_top[mine, RANK : 2 * RANK] = b_in[1] + b_in[2]
        ct_top[mine, 2 * RANK : 3 * RANK] = (b_in[3] + b_in[4]) + (b_in[5] + b_in[6])
        each(lambda d: gather_top(d).start())

    def dense(i, c):
        cut = pl.ds(pl.multiple_of(i * STEP, STEP), STEP)
        right = xr[:, cut]
        total = dot(tt[:, FARW:ALLW], vt[FARW:ALLW, cut])
        for r in range(0, PTS, LEAF):
            total = total + dot(xt[:, r : r + LEAF], gauss(xlt[r : r + LEAF, :], right))
        yt[:, cut] = total
        for when, what in ((SEND_NEAR, send_near), (SEND_LOW, send_low), (SEND_TOP, send_top)):
            pl.when(i == when)(what)
        return c

    lax.fori_loop(0, PTS // STEP, dense, 0)

    each(lambda d: gather_low(d).wait_recv())
    for j in range(LOW):
        scale = 1.0 / math.sqrt(PTS * 2.0**j)
        tt[:, TOPW + j * RANK : TOPW + (j + 1) * RANK] = mix(ct_low[:, j * RANK : (j + 1) * RANK], coupling[2 + j], scale)
    for c in range(0, PTS, LEAF):
        cut = slice(c, c + LEAF)
        yt[:, cut] += dot(tt[:, TOPW:FARW], vt[TOPW:FARW, cut])
    each(lambda d: gather_top(d).wait_recv())
    for j in range(TOP):
        scale = 1.0 / math.sqrt(PTS * 2.0 ** (FIRST + j))
        tt[:, j * RANK : (j + 1) * RANK] = mix(ct_top[:, j * RANK : (j + 1) * RANK], coupling[2 + FIRST + j], scale)
    for c in range(0, PTS, LEAF):
        cut = slice(c, c + LEAF)
        out[cut, :] = (yt[:, cut] + dot(tt[:, 0:TOPW], vt[0:TOPW, cut])).T

    each(lambda d: scatter_top(d).wait_send())
    each(lambda d: scatter_low(d).wait_send())
    each(lambda d: gather_top(d).wait_send())
    each(lambda d: gather_low(d).wait_send())
    for m in range(1, 4):
        near_top(m).wait_send()
        near_low(m).wait_send()
    for m in range(1, 8):
        far_top(m).wait_send()


def per_device(points, rhs, order, anchors, coupling):
    given = (points[0, 0], rhs[0, 0], order[0, 0].reshape(PTS // 128, 128), anchors[0, 0], coupling[0, 0])
    scratch = [(a.shape, a.dtype) for a in given] + [
        ((DEPTH, PTS), bf16),
        ((PTS, DEPTH), bf16),
        ((ALLW, DEPTH), bf16),
        ((RHS, PTS), bf16),
        ((ALLW, PTS), bf16),
        ((RHS, PTS), f32),
        ((RHS, ALLW), bf16),
        ((1, PTS), f32),
        ((RHS, TOPW), f32),
        ((RHS, LOWW), f32),
        ((RHS, 2 * RANK), f32),
        ((LO, ROWS, TOPW), f32),
        ((LO, ROWS, LOWW), f32),
        ((ROWS, TOPW), f32),
        ((ROWS, 2 * RANK), f32),
        ((3, ROWS, TOPW), f32),
        ((3, ROWS, RANK), f32),
        ((ROWS, TOPW), f32),
        ((7, ROWS, RANK), f32),
        ((RHS, TOPW), f32),
        ((RHS, LOWW), f32),
        ((LO, ROWS, LOWW), f32),
    ]
    sems = [pltpu.SemaphoreType.DMA((n,)) for n in [5] + [LO] * 8 + [3] * 4 + [7] * 2]
    out = pl.pallas_call(
        body,
        out_shape=pltpu.VMEM((PTS, RHS), f32),
        in_specs=[pl.BlockSpec(memory_space=pltpu.HBM)] * 5,
        out_specs=pl.BlockSpec(memory_space=pltpu.VMEM),
        scratch_shapes=[pltpu.VMEM(s, d) for s, d in scratch] + sems,
        compiler_params=pltpu.CompilerParams(
            collective_id=0, has_side_effects=True, vmem_limit_bytes=60 * 2**20
        ),
        name="hodlr",
    )(*given)
    return out[None, None]


def solution(mesh):
    return jax.shard_map(
        per_device,
        mesh=mesh,
        in_specs=(
            P("hi", "lo", None, None),
            P("hi", "lo", None, None),
            P("hi", "lo", None),
            P("hi", "lo", None, None, None),
            P("hi", "lo", None, None, None),
        ),
        out_specs=P("hi", "lo", None, None),
        check_vma=False,
    )
```

```python
import math

import jax
import jax.numpy as jnp
from jax import lax
from jax.experimental import pallas as pl
from jax.experimental.pallas import tpu as pltpu
from jax.sharding import PartitionSpec as P

bf16 = jnp.bfloat16
f32 = jnp.float32
MESH = pl.DeviceIdType.MESH

WIDTH = 64
RANK = 128
RHS = 128
PTS = 4096
LEAF = 2048
SIDE = 4
LO = 16
FIRST = 6
TOP, LOW = 3, 6
INSIDE = 4
TOPW, LOWW = TOP * RANK, LOW * RANK
FARW = TOPW + LOWW
ALLW = FARW + 2 * RANK
ROWS = RHS // LO
DEPTH = 128
EXPONENT = math.log2(math.e) * 4.0 / WIDTH
SIGN = 32.0
COLS = 1024
STEP = 512
EARLY = 2
EARLY_AT = (2, 3, 3, 4, 6)
LATE_AT = (-2, -1, 0, 1, 5)


def dot(a, b):
    return jnp.dot(a, b, preferred_element_type=f32)


def dot_nt(a, b, **kw):
    return lax.dot_general(a, b, (((1,), (1,)), ((), ())), preferred_element_type=f32, **kw)


def gauss(a, b):
    return jnp.exp2(dot(a, b) * EXPONENT).astype(bf16)


def flip(index, mask):
    for bit in range(5):
        if mask >> bit & 1:
            step = 1 << bit
            index = index + step * (1 - 2 * (index // step % 2))
    return index


def split3(value):
    first = value.astype(bf16).astype(f32)
    rest = value - first
    second = rest.astype(bf16).astype(f32)
    return first, second, rest - second


def extended(cols, sign, offset, mirrored):
    n = cols.shape[1]
    half = -0.5 * jnp.sum(cols * cols, axis=0, keepdims=True)
    first, second, third = split3(half)
    row = lax.broadcasted_iota(jnp.int32, (16, n), 0)
    base = 3 if mirrored else 0
    block = jnp.where((row < 6), 1.0, 0.0)
    block = jnp.where(row == base, first, block)
    block = jnp.where(row == base + 1, second, block)
    block = jnp.where(row == base + 2, third, block)
    block = jnp.where(row == 6, sign, block)
    return jnp.where(row == 7, offset, block)


def body(
    points_in, rhs_in, order_in, anchors_in, coupling_in, out,
    points, rhs, order, anchors, coupling,
    xr, xlt, zlt, xt, vt, yt, tt, srow,
    pt_top, pt_low, et, rs_top, rs_low, q_top, q_low, a_in, e_in, g_top, b_in, ct_top, ct_low, ag_low,
    in_s, su_s, su_r, sd_s, sd_r, gu_s, gu_r, gd_s, gd_r, a_s, a_r, e_s, e_r, b_s, b_r, ready,
):
    arriving = [
        pltpu.make_async_copy(src, dst, in_s.at[k])
        for k, (src, dst) in enumerate(
            ((points_in, points), (anchors_in, anchors), (rhs_in, rhs), (order_in, order), (coupling_in, coupling))
        )
    ]
    for piece in arriving:
        piece.start()

    lo, hi = lax.axis_index("lo"), lax.axis_index("hi")
    y, x = lo // SIDE, lo % SIDE
    mine = pl.ds(pl.multiple_of(ROWS * lo, ROWS), ROWS)

    def onward(d):
        return (y + d // SIDE) % SIDE * SIDE + (x + d % SIDE) % SIDE

    def rows_of(index):
        return pl.ds(pl.multiple_of(ROWS * index, ROWS), ROWS)

    def copy(src, dst, send, recv, where):
        return pltpu.make_async_remote_copy(
            src_ref=src, dst_ref=dst, send_sem=send, recv_sem=recv, device_id=where, device_id_type=MESH
        )

    def scatter(d, src, dst, send, recv):
        there = onward(d)
        return copy(src.at[rows_of(there)], dst.at[lo], send.at[d], recv.at[d], {"lo": there, "hi": hi})

    def scatter_top(d):
        return scatter(d, pt_top, rs_top, su_s, su_r)

    def scatter_low(d):
        return scatter(d, pt_low, rs_low, sd_s, sd_r)

    def gather_top(d):
        return copy(ct_top.at[mine], ct_top.at[mine], gu_s.at[d], gu_r.at[d], {"lo": onward(d), "hi": hi})

    def gather_low(d):
        there = onward(d)
        return copy(ag_low.at[there], ct_low.at[mine], gd_s.at[d], gd_r.at[d], {"lo": there, "hi": hi})

    def near_top(m):
        return copy(q_top, a_in.at[m - 1], a_s.at[m - 1], a_r.at[m - 1], {"lo": lo, "hi": flip(hi, m)})

    def near_low(m):
        src = q_low.at[:, 0:RANK] if m == 1 else q_low.at[:, RANK : 2 * RANK]
        return copy(src, e_in.at[m - 1], e_s.at[m - 1], e_r.at[m - 1], {"lo": lo, "hi": flip(hi, m)})

    def far_top(m):
        level = 0 if m == 1 else 1 if m < 4 else 2
        src = g_top.at[:, level * RANK : (level + 1) * RANK]
        return copy(src, b_in.at[m - 1], b_s.at[m - 1], b_r.at[m - 1], {"lo": lo, "hi": flip(hi, 4 * m)})

    def each(fn):
        def step(d, c):
            fn(d)
            return c

        lax.fori_loop(1, LO, step, 0)

    barrier = pltpu.get_barrier_semaphore()
    each(lambda d: pl.semaphore_signal(barrier, inc=1, device_id={"lo": onward(d), "hi": hi}, device_id_type=MESH))
    for m in range(1, 4):
        pl.semaphore_signal(barrier, inc=1, device_id={"lo": lo, "hi": flip(hi, m)}, device_id_type=MESH)
    quad = hi // 4

    def upper(m):
        return quad // (1 << (m.bit_length() - 1)) % 2 == 1

    for m in range(1, 8):

        @pl.when(jnp.logical_not(upper(m)))
        def _():
            pl.semaphore_signal(barrier, inc=1, device_id={"lo": lo, "hi": flip(hi, 4 * m)}, device_id_type=MESH)

    when_at = [jnp.where(quad < EARLY, a, b) for a, b in zip(EARLY_AT, LATE_AT)]

    pad = DEPTH - WIDTH - 16
    arriving[0].wait()
    for c in range(0, PTS, COLS):
        cut = slice(c, c + COLS)
        xr[0:WIDTH, cut] = points[:, cut]
        xr[WIDTH : WIDTH + 16, cut] = extended(points[:, cut].astype(f32), 0.0, 1.0, False).astype(bf16)
        xr[WIDTH + 16 : DEPTH, cut] = jnp.zeros((pad, COLS), bf16)

    sets = [2 + FIRST + j for j in range(TOP)] + [2 + j for j in range(LOW)] + [0, 1]

    def anchor_rows(first, last):
        for k in range(first, last):
            s = sets[k]
            cols = anchors[s].astype(f32)
            sign = SIGN * (2 * s - 1) if s < 2 else 0.0
            offset = -SIGN * SIGN if s < 2 else 0.0
            left = jnp.concatenate([cols, extended(cols, sign, offset, True), jnp.zeros((pad, RANK), f32)], 0)
            zlt[k * RANK : (k + 1) * RANK, :] = left.T.astype(bf16)

    arriving[1].wait()
    anchor_rows(0, TOP)
    arriving[2].wait()
    for c in range(0, PTS, COLS):
        cut = slice(c, c + COLS)
        xt[:, cut] = rhs[cut, :].T

    def basis(first, width, piece, sums):
        total = None
        for c in range(0, PTS, piece):
            cut = slice(c, c + piece)
            tile = gauss(zlt[first : first + width], xr[:, cut])
            vt[first : first + width, cut] = tile
            part = dot_nt(xt[:, cut], tile)
            total = part if total is None else total + part
        sums[...] = total

    basis(0, TOPW, 1024, pt_top)
    pl.semaphore_wait(barrier, LO - 1 + 3 + quad)
    for m in range(1, 8):

        @pl.when(upper(m))
        def _():
            pl.semaphore_signal(ready, inc=1, device_id={"lo": lo, "hi": flip(hi, 4 * m)}, device_id_type=MESH)

    each(lambda d: scatter_top(d).start())
    rs_top[lo] = pt_top[mine, :]
    anchor_rows(TOP, TOP + LOW)
    basis(TOPW, LOWW, 1024, pt_low)
    each(lambda d: scatter_low(d).start())
    rs_low[lo] = pt_low[mine, :]

    def send_near():
        each(lambda d: scatter_top(d).wait_recv())
        total = rs_top[0]
        for g in range(1, LO):
            total = total + rs_top[g]
        q_top[...] = total
        for m in range(1, 4):
            near_top(m).start()

    def send_far():
        for m in range(1, 4):
            near_top(m).wait_recv()
        g_top[...] = (q_top[...] + a_in[0]) + (a_in[1] + a_in[2])
        for m in range(1, 8):
            pl.when(upper(m))(far_top(m).start)

        @pl.when(quad < 7)
        def _():
            pl.semaphore_wait(ready, 7 - quad)

        for m in range(1, 8):
            pl.when(jnp.logical_not(upper(m)))(far_top(m).start)

    pl.when(when_at[0] == -2)(send_near)

    arriving[3].wait()
    lane_hot, row_hot = [], []
    for k in range(LEAF // 128, PTS // 128):
        line = order[k : k + 1, :]
        lane_hot.append(jnp.where(lax.broadcasted_iota(jnp.int32, (128, 128), 0) == (line & 127), 1.0, 0.0).astype(bf16))
        row_hot.append(jnp.where(lax.broadcasted_iota(jnp.int32, (32, 128), 0) == (line >> 7), 1.0, 0.0).astype(bf16))
    in_second = dot_nt(jnp.concatenate(row_hot, 1), jnp.concatenate(lane_hot, 1))
    signs = (2.0 * in_second - 1.0) * SIGN
    for k in range(PTS // 128):
        srow[:, k * 128 : (k + 1) * 128] = signs[k : k + 1, :]
    for c in range(0, PTS, COLS):
        cut = slice(c, c + COLS)
        cols = points[:, cut].astype(f32)
        xr[WIDTH : WIDTH + 16, cut] = extended(cols, srow[:, cut], 1.0, False).astype(bf16)
        left = jnp.concatenate([cols, extended(cols, srow[:, cut], -SIGN * SIGN, True), jnp.zeros((pad, COLS), f32)], 0)
        xlt[cut, :] = left.T.astype(bf16)
    anchor_rows(TOP + LOW, TOP + LOW + 2)

    pl.when(when_at[1] == -1)(send_far)
    basis(FARW, 2 * RANK, 2048, et)
    arriving[4].wait()

    def mix(coef, core, scale):
        return dot_nt(coef * scale, core, precision=lax.Precision.HIGHEST).astype(bf16)

    for a in range(2):
        coef = et[:, (1 - a) * RANK : (2 - a) * RANK]
        tt[:, FARW + a * RANK : FARW + (a + 1) * RANK] = mix(coef, coupling[a], 1.0 / math.sqrt(LEAF))

    def sum_low():
        each(lambda d: scatter_low(d).wait_recv())
        lanes = slice(INSIDE * RANK, LOWW)
        total = rs_low[0, :, lanes]
        for g in range(1, LO):
            total = total + rs_low[g, :, lanes]
        q_low[...] = total
        for m in range(1, 4):
            near_low(m).start()
        for j in range(INSIDE):
            lanes = slice(j * RANK, (j + 1) * RANK)
            sums = [rs_low[g, :, lanes] for g in range(LO)]
            for _ in range(j):
                sums = [sums[2 * k] + sums[2 * k + 1] for k in range(len(sums) // 2)]
            for g in range(LO):
                ag_low[g, :, lanes] = sums[(g >> j) ^ 1]

    def send_low():
        for m in range(1, 4):
            near_low(m).wait_recv()
        fourth, fifth = e_in[0], e_in[1] + e_in[2]
        for g in range(LO):
            ag_low[g, :, INSIDE * RANK : (INSIDE + 1) * RANK] = fourth
            ag_low[g, :, (INSIDE + 1) * RANK : LOWW] = fifth
        each(lambda d: gather_low(d).start())
        ct_low[mine, :] = ag_low[lo]

    def send_top():
        for m in range(1, 8):
            far_top(m).wait_recv()
        ct_top[mine, 0:RANK] = b_in[0]
        ct_top[mine, RANK : 2 * RANK] = b_in[1] + b_in[2]
        ct_top[mine, 2 * RANK : 3 * RANK] = (b_in[3] + b_in[4]) + (b_in[5] + b_in[6])
        each(lambda d: gather_top(d).start())

    def dense(i, c):
        for at, what in zip(when_at, (send_near, send_far, sum_low, send_low, send_top)):
            pl.when(i == at)(what)
        cut = pl.ds(pl.multiple_of(i * STEP, STEP), STEP)
        right = xr[:, cut]
        total = dot(tt[:, FARW:ALLW], vt[FARW:ALLW, cut])
        for r in range(0, PTS, LEAF):
            total = total + dot(xt[:, r : r + LEAF], gauss(xlt[r : r + LEAF, :], right))
        yt[:, cut] = total
        return c

    lax.fori_loop(0, PTS // STEP, dense, 0)

    each(lambda d: gather_low(d).wait_recv())
    for j in range(LOW):
        scale = 1.0 / math.sqrt(PTS * 2.0**j)
        tt[:, TOPW + j * RANK : TOPW + (j + 1) * RANK] = mix(ct_low[:, j * RANK : (j + 1) * RANK], coupling[2 + j], scale)
    for c in range(0, PTS, LEAF):
        cut = slice(c, c + LEAF)
        yt[:, cut] += dot(tt[:, TOPW:FARW], vt[TOPW:FARW, cut])
    each(lambda d: gather_top(d).wait_recv())
    for j in range(TOP):
        scale = 1.0 / math.sqrt(PTS * 2.0 ** (FIRST + j))
        tt[:, j * RANK : (j + 1) * RANK] = mix(ct_top[:, j * RANK : (j + 1) * RANK], coupling[2 + FIRST + j], scale)
    for c in range(0, PTS, LEAF):
        cut = slice(c, c + LEAF)
        out[cut, :] = (yt[:, cut] + dot(tt[:, 0:TOPW], vt[0:TOPW, cut])).T

    each(lambda d: scatter_top(d).wait_send())
    each(lambda d: scatter_low(d).wait_send())
    each(lambda d: gather_top(d).wait_send())
    each(lambda d: gather_low(d).wait_send())
    for m in range(1, 4):
        near_top(m).wait_send()
        near_low(m).wait_send()
    for m in range(1, 8):
        far_top(m).wait_send()


def per_device(points, rhs, order, anchors, coupling):
    given = (points[0, 0], rhs[0, 0], order[0, 0].reshape(PTS // 128, 128), anchors[0, 0], coupling[0, 0])
    scratch = [(a.shape, a.dtype) for a in given] + [
        ((DEPTH, PTS), bf16),
        ((PTS, DEPTH), bf16),
        ((ALLW, DEPTH), bf16),
        ((RHS, PTS), bf16),
        ((ALLW, PTS), bf16),
        ((RHS, PTS), f32),
        ((RHS, ALLW), bf16),
        ((1, PTS), f32),
        ((RHS, TOPW), f32),
        ((RHS, LOWW), f32),
        ((RHS, 2 * RANK), f32),
        ((LO, ROWS, TOPW), f32),
        ((LO, ROWS, LOWW), f32),
        ((ROWS, TOPW), f32),
        ((ROWS, 2 * RANK), f32),
        ((3, ROWS, TOPW), f32),
        ((3, ROWS, RANK), f32),
        ((ROWS, TOPW), f32),
        ((7, ROWS, RANK), f32),
        ((RHS, TOPW), f32),
        ((RHS, LOWW), f32),
        ((LO, ROWS, LOWW), f32),
    ]
    sems = [pltpu.SemaphoreType.DMA((n,)) for n in [5] + [LO] * 8 + [3] * 4 + [7] * 2]
    sems.append(pltpu.SemaphoreType.REGULAR)
    out = pl.pallas_call(
        body,
        out_shape=pltpu.VMEM((PTS, RHS), f32),
        in_specs=[pl.BlockSpec(memory_space=pltpu.HBM)] * 5,
        out_specs=pl.BlockSpec(memory_space=pltpu.VMEM),
        scratch_shapes=[pltpu.VMEM(s, d) for s, d in scratch] + sems,
        compiler_params=pltpu.CompilerParams(
            collective_id=0, has_side_effects=True, vmem_limit_bytes=60 * 2**20
        ),
        name="hodlr",
    )(*given)
    return out[None, None]


def solution(mesh):
    return jax.shard_map(
        per_device,
        mesh=mesh,
        in_specs=(
            P("hi", "lo", None, None),
            P("hi", "lo", None, None),
            P("hi", "lo", None),
            P("hi", "lo", None, None, None),
            P("hi", "lo", None, None, None),
        ),
        out_specs=P("hi", "lo", None, None),
        check_vma=False,
    )
```

```python
import math

import jax
import jax.numpy as jnp
from jax import lax
from jax.experimental import pallas as pl
from jax.experimental.pallas import tpu as pltpu
from jax.sharding import PartitionSpec as P

bf16 = jnp.bfloat16
f32 = jnp.float32
MESH = pl.DeviceIdType.MESH

WIDTH = 64
RANK = 128
RHS = 128
PTS = 4096
LEAF = 2048
SIDE = 4
LO = 16
FIRST = 6
TOP, LOW = 3, 6
INSIDE = 4
TOPW, LOWW = TOP * RANK, LOW * RANK
FARW = TOPW + LOWW
ALLW = FARW + 2 * RANK
ROWS = RHS // LO
DEPTH = 128
EXPONENT = math.log2(math.e) * 4.0 / WIDTH
SIGN = 32.0
COLS = 1024
STEP = 512
PLACES = (
    (2, 3, 5, 3, 4, 7),
    (1, 2, 4, 2, 3, 7),
    (1, 2, 3, 2, 3, 6),
    (-1, 0, 2, 1, 2, 6),
    (-1, 0, 2, 3, 4, 6),
    (-3, -1, 1, 2, 4, 6),
)
WAYS = (10, 6, 9, 11, 14, 2, 8, 5, 7, 13, 15, 1, 3, 4, 12)


def dot(a, b):
    return jnp.dot(a, b, preferred_element_type=f32)


def dot_nt(a, b, **kw):
    return lax.dot_general(a, b, (((1,), (1,)), ((), ())), preferred_element_type=f32, **kw)


def gauss(a, b):
    return jnp.exp2(dot(a, b) * EXPONENT).astype(bf16)


def flip(index, mask):
    for bit in range(5):
        if mask >> bit & 1:
            step = 1 << bit
            index = index + step * (1 - 2 * (index // step % 2))
    return index


def split3(value):
    first = value.astype(bf16).astype(f32)
    rest = value - first
    second = rest.astype(bf16).astype(f32)
    return first, second, rest - second


def extended(cols, sign, offset, mirrored):
    n = cols.shape[1]
    half = -0.5 * jnp.sum(cols * cols, axis=0, keepdims=True)
    first, second, third = split3(half)
    row = lax.broadcasted_iota(jnp.int32, (16, n), 0)
    base = 3 if mirrored else 0
    block = jnp.where((row < 6), 1.0, 0.0)
    block = jnp.where(row == base, first, block)
    block = jnp.where(row == base + 1, second, block)
    block = jnp.where(row == base + 2, third, block)
    block = jnp.where(row == 6, sign, block)
    return jnp.where(row == 7, offset, block)


def body(
    points_in, rhs_in, order_in, anchors_in, coupling_in, out,
    points, rhs, order, anchors, coupling,
    xr, xlt, zlt, xt, vt, yt, tt, srow,
    pt_top, pt_low, et, rs_top, rs_low, q_top, q_low, a_in, e_in, g_top, b_in, ct_top, ct_low, ag_low,
    in_s, su_s, su_r, sd_s, sd_r, gu_s, gu_r, gd_s, gd_r, a_s, a_r, e_s, e_r, b_s, b_r, ready,
):
    arriving = [
        pltpu.make_async_copy(src, dst, in_s.at[k])
        for k, (src, dst) in enumerate(
            ((points_in, points), (anchors_in, anchors), (rhs_in, rhs), (order_in, order), (coupling_in, coupling))
        )
    ]
    for piece in arriving:
        piece.start()

    lo, hi = lax.axis_index("lo"), lax.axis_index("hi")
    y, x = lo // SIDE, lo % SIDE
    mine = pl.ds(pl.multiple_of(ROWS * lo, ROWS), ROWS)

    def onward(d):
        return (y + d // SIDE) % SIDE * SIDE + (x + d % SIDE) % SIDE

    def rows_of(index):
        return pl.ds(pl.multiple_of(ROWS * index, ROWS), ROWS)

    def copy(src, dst, send, recv, where):
        return pltpu.make_async_remote_copy(
            src_ref=src, dst_ref=dst, send_sem=send, recv_sem=recv, device_id=where, device_id_type=MESH
        )

    def scatter(d, src, dst, send, recv):
        there = onward(d)
        return copy(src.at[rows_of(there)], dst.at[lo], send.at[d], recv.at[d], {"lo": there, "hi": hi})

    def scatter_top(d):
        return scatter(d, pt_top, rs_top, su_s, su_r)

    def scatter_low(d):
        return scatter(d, pt_low, rs_low, sd_s, sd_r)

    def gather_top(d):
        return copy(ct_top.at[mine], ct_top.at[mine], gu_s.at[d], gu_r.at[d], {"lo": onward(d), "hi": hi})

    def gather_low(d):
        there = onward(d)
        return copy(ag_low.at[there], ct_low.at[mine], gd_s.at[d], gd_r.at[d], {"lo": there, "hi": hi})

    def near_top(m):
        return copy(q_top, a_in.at[m - 1], a_s.at[m - 1], a_r.at[m - 1], {"lo": lo, "hi": flip(hi, m)})

    def near_low(m):
        src = q_low.at[:, 0:RANK] if m == 1 else q_low.at[:, RANK : 2 * RANK]
        return copy(src, e_in.at[m - 1], e_s.at[m - 1], e_r.at[m - 1], {"lo": lo, "hi": flip(hi, m)})

    def far_top(m):
        level = 0 if m == 1 else 1 if m < 4 else 2
        src = g_top.at[:, level * RANK : (level + 1) * RANK]
        return copy(src, b_in.at[m - 1], b_s.at[m - 1], b_r.at[m - 1], {"lo": lo, "hi": flip(hi, 4 * m)})

    def each(fn):
        def step(d, c):
            fn(d)
            return c

        lax.fori_loop(1, LO, step, 0)

    barrier = pltpu.get_barrier_semaphore()
    each(lambda d: pl.semaphore_signal(barrier, inc=1, device_id={"lo": onward(d), "hi": hi}, device_id_type=MESH))
    for m in range(1, 4):
        pl.semaphore_signal(barrier, inc=1, device_id={"lo": lo, "hi": flip(hi, m)}, device_id_type=MESH)
    quad = hi // 4

    def upper(m):
        return quad // (1 << (m.bit_length() - 1)) % 2 == 1

    for m in range(1, 8):

        @pl.when(jnp.logical_not(upper(m)))
        def _():
            pl.semaphore_signal(barrier, inc=1, device_id={"lo": lo, "hi": flip(hi, 4 * m)}, device_id_type=MESH)

    rank = jnp.minimum(quad, 4) + jnp.where(x + y < 2, 0, jnp.where(quad == 3, 2, 1))
    rank = jnp.where(lo + hi == 0, 3, rank)
    places = []
    for choice in zip(*PLACES):
        place = choice[-1]
        for k in range(len(choice) - 2, -1, -1):
            place = jnp.where(rank == k, choice[k], place)
        places.append(place)

    pad = DEPTH - WIDTH - 16
    arriving[0].wait()
    for c in range(0, PTS, COLS):
        cut = slice(c, c + COLS)
        xr[0:WIDTH, cut] = points[:, cut]
        xr[WIDTH : WIDTH + 16, cut] = extended(points[:, cut].astype(f32), 0.0, 1.0, False).astype(bf16)
        xr[WIDTH + 16 : DEPTH, cut] = jnp.zeros((pad, COLS), bf16)

    sets = [2 + FIRST + j for j in range(TOP)] + [2 + j for j in range(LOW)] + [0, 1]

    def anchor_rows(first, last):
        for k in range(first, last):
            s = sets[k]
            cols = anchors[s].astype(f32)
            sign = SIGN * (2 * s - 1) if s < 2 else 0.0
            offset = -SIGN * SIGN if s < 2 else 0.0
            left = jnp.concatenate([cols, extended(cols, sign, offset, True), jnp.zeros((pad, RANK), f32)], 0)
            zlt[k * RANK : (k + 1) * RANK, :] = left.T.astype(bf16)

    arriving[1].wait()
    anchor_rows(0, TOP)
    arriving[2].wait()
    for c in range(0, PTS, COLS):
        cut = slice(c, c + COLS)
        xt[:, cut] = rhs[cut, :].T

    def basis(first, width, piece, sums):
        total = None
        for c in range(0, PTS, piece):
            cut = slice(c, c + piece)
            tile = gauss(zlt[first : first + width], xr[:, cut])
            vt[first : first + width, cut] = tile
            part = dot_nt(xt[:, cut], tile)
            total = part if total is None else total + part
        sums[...] = total

    basis(0, TOPW, 1024, pt_top)
    pl.semaphore_wait(barrier, LO - 1 + 3 + quad)
    for m in range(1, 8):

        @pl.when(upper(m))
        def _():
            pl.semaphore_signal(ready, inc=1, device_id={"lo": lo, "hi": flip(hi, 4 * m)}, device_id_type=MESH)

    for d in WAYS:
        scatter_top(d).start()
    rs_top[lo] = pt_top[mine, :]
    anchor_rows(TOP, TOP + LOW)
    basis(TOPW, LOWW, 1024, pt_low)
    def send_near():
        each(lambda d: scatter_top(d).wait_recv())
        total = rs_top[0]
        for g in range(1, LO):
            total = total + rs_top[g]
        q_top[...] = total
        for m in range(1, 4):
            near_top(m).start()

    def send_far():
        for m in range(1, 4):
            near_top(m).wait_recv()
        g_top[...] = (q_top[...] + a_in[0]) + (a_in[1] + a_in[2])
        for m in range(1, 8):
            pl.when(upper(m))(far_top(m).start)

    def send_up():
        @pl.when(quad < 7)
        def _():
            pl.semaphore_wait(ready, 7 - quad)

        for m in range(1, 8):
            pl.when(jnp.logical_not(upper(m)))(far_top(m).start)

    pl.when(places[0] == -3)(send_near)
    start_low = lambda: each(lambda d: scatter_low(d).start())
    pl.when(rank != 4)(start_low)
    rs_low[lo] = pt_low[mine, :]

    arriving[3].wait()
    lane_hot, row_hot = [], []
    for k in range(LEAF // 128, PTS // 128):
        line = order[k : k + 1, :]
        lane_hot.append(jnp.where(lax.broadcasted_iota(jnp.int32, (128, 128), 0) == (line & 127), 1.0, 0.0).astype(bf16))
        row_hot.append(jnp.where(lax.broadcasted_iota(jnp.int32, (32, 128), 0) == (line >> 7), 1.0, 0.0).astype(bf16))
    in_second = dot_nt(jnp.concatenate(row_hot, 1), jnp.concatenate(lane_hot, 1))
    signs = (2.0 * in_second - 1.0) * SIGN
    for k in range(PTS // 128):
        srow[:, k * 128 : (k + 1) * 128] = signs[k : k + 1, :]
    for c in range(0, PTS, COLS):
        cut = slice(c, c + COLS)
        cols = points[:, cut].astype(f32)
        xr[WIDTH : WIDTH + 16, cut] = extended(cols, srow[:, cut], 1.0, False).astype(bf16)
        left = jnp.concatenate([cols, extended(cols, srow[:, cut], -SIGN * SIGN, True), jnp.zeros((pad, COLS), f32)], 0)
        xlt[cut, :] = left.T.astype(bf16)
    anchor_rows(TOP + LOW, TOP + LOW + 2)

    pl.when(places[0] == -1)(send_near)
    pl.when(rank == 4)(start_low)
    pl.when(places[1] == -1)(send_far)
    basis(FARW, 2 * RANK, 2048, et)
    arriving[4].wait()

    def mix(coef, core, scale):
        return dot_nt(coef * scale, core, precision=lax.Precision.HIGHEST).astype(bf16)

    for a in range(2):
        coef = et[:, (1 - a) * RANK : (2 - a) * RANK]
        tt[:, FARW + a * RANK : FARW + (a + 1) * RANK] = mix(coef, coupling[a], 1.0 / math.sqrt(LEAF))

    def sum_low():
        each(lambda d: scatter_low(d).wait_recv())
        lanes = slice(INSIDE * RANK, LOWW)
        total = rs_low[0, :, lanes]
        for g in range(1, LO):
            total = total + rs_low[g, :, lanes]
        q_low[...] = total
        for m in range(1, 4):
            near_low(m).start()
        for j in range(INSIDE):
            lanes = slice(j * RANK, (j + 1) * RANK)
            sums = [rs_low[g, :, lanes] for g in range(LO)]
            for _ in range(j):
                sums = [sums[2 * k] + sums[2 * k + 1] for k in range(len(sums) // 2)]
            for g in range(LO):
                ag_low[g, :, lanes] = sums[(g >> j) ^ 1]

    def send_low():
        for m in range(1, 4):
            near_low(m).wait_recv()
        fourth, fifth = e_in[0], e_in[1] + e_in[2]
        for g in range(LO):
            ag_low[g, :, INSIDE * RANK : (INSIDE + 1) * RANK] = fourth
            ag_low[g, :, (INSIDE + 1) * RANK : LOWW] = fifth
        each(lambda d: gather_low(d).start())
        ct_low[mine, :] = ag_low[lo]

    def send_top():
        for m in range(1, 8):
            far_top(m).wait_recv()
        ct_top[mine, 0:RANK] = b_in[0]
        ct_top[mine, RANK : 2 * RANK] = b_in[1] + b_in[2]
        ct_top[mine, 2 * RANK : 3 * RANK] = (b_in[3] + b_in[4]) + (b_in[5] + b_in[6])
        for d in WAYS:
            gather_top(d).start()

    def dense(i, c):
        for at, what in zip(places, (send_near, send_far, send_up, sum_low, send_low, send_top)):
            pl.when(i == at)(what)
        cut = pl.ds(pl.multiple_of(i * STEP, STEP), STEP)
        right = xr[:, cut]
        total = dot(tt[:, FARW:ALLW], vt[FARW:ALLW, cut])
        for r in range(0, PTS, LEAF):
            total = total + dot(xt[:, r : r + LEAF], gauss(xlt[r : r + LEAF, :], right))
        yt[:, cut] = total
        return c

    lax.fori_loop(0, PTS // STEP, dense, 0)

    each(lambda d: gather_low(d).wait_recv())
    for j in range(LOW):
        scale = 1.0 / math.sqrt(PTS * 2.0**j)
        tt[:, TOPW + j * RANK : TOPW + (j + 1) * RANK] = mix(ct_low[:, j * RANK : (j + 1) * RANK], coupling[2 + j], scale)
    for c in range(0, PTS, LEAF):
        cut = slice(c, c + LEAF)
        yt[:, cut] += dot(tt[:, TOPW:FARW], vt[TOPW:FARW, cut])
    each(lambda d: scatter_top(d).wait_send())
    each(lambda d: scatter_low(d).wait_send())
    each(lambda d: gather_low(d).wait_send())
    for m in range(1, 4):
        near_top(m).wait_send()
        near_low(m).wait_send()
    for m in range(1, 8):
        far_top(m).wait_send()
    each(lambda d: gather_top(d).wait_send())
    each(lambda d: gather_top(d).wait_recv())
    for j in range(TOP):
        scale = 1.0 / math.sqrt(PTS * 2.0 ** (FIRST + j))
        tt[:, j * RANK : (j + 1) * RANK] = mix(ct_top[:, j * RANK : (j + 1) * RANK], coupling[2 + FIRST + j], scale)
    for c in range(0, PTS, LEAF):
        cut = slice(c, c + LEAF)
        out[cut, :] = (yt[:, cut] + dot(tt[:, 0:TOPW], vt[0:TOPW, cut])).T


def per_device(points, rhs, order, anchors, coupling):
    given = (points[0, 0], rhs[0, 0], order[0, 0].reshape(PTS // 128, 128), anchors[0, 0], coupling[0, 0])
    scratch = [(a.shape, a.dtype) for a in given] + [
        ((DEPTH, PTS), bf16),
        ((PTS, DEPTH), bf16),
        ((ALLW, DEPTH), bf16),
        ((RHS, PTS), bf16),
        ((ALLW, PTS), bf16),
        ((RHS, PTS), f32),
        ((RHS, ALLW), bf16),
        ((1, PTS), f32),
        ((RHS, TOPW), f32),
        ((RHS, LOWW), f32),
        ((RHS, 2 * RANK), f32),
        ((LO, ROWS, TOPW), f32),
        ((LO, ROWS, LOWW), f32),
        ((ROWS, TOPW), f32),
        ((ROWS, 2 * RANK), f32),
        ((3, ROWS, TOPW), f32),
        ((3, ROWS, RANK), f32),
        ((ROWS, TOPW), f32),
        ((7, ROWS, RANK), f32),
        ((RHS, TOPW), f32),
        ((RHS, LOWW), f32),
        ((LO, ROWS, LOWW), f32),
    ]
    sems = [pltpu.SemaphoreType.DMA((n,)) for n in [5] + [LO] * 8 + [3] * 4 + [7] * 2]
    sems.append(pltpu.SemaphoreType.REGULAR)
    out = pl.pallas_call(
        body,
        out_shape=pltpu.VMEM((PTS, RHS), f32),
        in_specs=[pl.BlockSpec(memory_space=pltpu.HBM)] * 5,
        out_specs=pl.BlockSpec(memory_space=pltpu.VMEM),
        scratch_shapes=[pltpu.VMEM(s, d) for s, d in scratch] + sems,
        compiler_params=pltpu.CompilerParams(
            collective_id=0, has_side_effects=True, vmem_limit_bytes=60 * 2**20
        ),
        name="hodlr",
    )(*given)
    return out[None, None]


def solution(mesh):
    return jax.shard_map(
        per_device,
        mesh=mesh,
        in_specs=(
            P("hi", "lo", None, None),
            P("hi", "lo", None, None),
            P("hi", "lo", None),
            P("hi", "lo", None, None, None),
            P("hi", "lo", None, None, None),
        ),
        out_specs=P("hi", "lo", None, None),
        check_vma=False,
    )
```

```python
import math

import jax
import jax.numpy as jnp
from jax import lax
from jax.experimental import pallas as pl
from jax.experimental.pallas import tpu as pltpu
from jax.sharding import PartitionSpec as P

bf16 = jnp.bfloat16
f32 = jnp.float32
MESH = pl.DeviceIdType.MESH

WIDTH = 64
RANK = 128
RHS = 128
PTS = 4096
LEAF = 2048
SIDE = 4
LO = 16
FIRST = 6
TOP, LOW = 3, 6
INSIDE = 4
TOPW, LOWW = TOP * RANK, LOW * RANK
FARW = TOPW + LOWW
ALLW = FARW + 2 * RANK
ROWS = RHS // LO
DEPTH = 128
EXPONENT = math.log2(math.e) * 4.0 / WIDTH
SIGN = 32.0
COLS = 1024
STEP = 512
PLACES = (
    (2, 3, 5, 3, 4, 7),
    (1, 2, 4, 2, 3, 7),
    (1, 2, 3, 2, 3, 6),
    (-1, 0, 2, 1, 2, 6),
    (-1, 0, 2, 3, 4, 6),
    (-3, -1, 1, 2, 4, 6),
)
WAYS = (10, 6, 9, 11, 14, 2, 8, 5, 7, 13, 15, 1, 3, 4, 12)


def dot(a, b):
    return jnp.dot(a, b, preferred_element_type=f32)


def dot_nt(a, b, **kw):
    return lax.dot_general(a, b, (((1,), (1,)), ((), ())), preferred_element_type=f32, **kw)


def gauss(a, b):
    return jnp.exp2(dot(a, b) * EXPONENT).astype(bf16)


def flip(index, mask):
    for bit in range(5):
        if mask >> bit & 1:
            step = 1 << bit
            index = index + step * (1 - 2 * (index // step % 2))
    return index


def split3(value):
    first = value.astype(bf16).astype(f32)
    rest = value - first
    second = rest.astype(bf16).astype(f32)
    return first, second, rest - second


def extended(cols, sign, offset, mirrored):
    n = cols.shape[1]
    half = -0.5 * jnp.sum(cols * cols, axis=0, keepdims=True)
    first, second, third = split3(half)
    row = lax.broadcasted_iota(jnp.int32, (16, n), 0)
    base = 3 if mirrored else 0
    block = jnp.where((row < 6), 1.0, 0.0)
    block = jnp.where(row == base, first, block)
    block = jnp.where(row == base + 1, second, block)
    block = jnp.where(row == base + 2, third, block)
    block = jnp.where(row == 6, sign, block)
    return jnp.where(row == 7, offset, block)


def body(
    points_in, rhs_in, order_in, anchors_in, coupling_in, out,
    points, rhs, order, anchors, coupling,
    xr, xlt, zlt, xt, vt, yt, tt, srow,
    pt_top, pt_low, et, rs_top, rs_low, q_top, q_low, a_in, e_in, g_top, b_in, ct_top, ct_low, ag_low,
    in_s, su_s, su_r, sd_s, sd_r, gu_s, gu_r, gd_s, gd_r, a_s, a_r, e_s, e_r, b_s, b_r, ready,
):
    arriving = [
        pltpu.make_async_copy(src, dst, in_s.at[k])
        for k, (src, dst) in enumerate(
            ((points_in, points), (anchors_in, anchors), (rhs_in, rhs), (order_in, order), (coupling_in, coupling))
        )
    ]
    for piece in arriving:
        piece.start()

    lo, hi = lax.axis_index("lo"), lax.axis_index("hi")
    y, x = lo // SIDE, lo % SIDE
    mine = pl.ds(pl.multiple_of(ROWS * lo, ROWS), ROWS)

    def onward(d):
        return (y + d // SIDE) % SIDE * SIDE + (x + d % SIDE) % SIDE

    def rows_of(index):
        return pl.ds(pl.multiple_of(ROWS * index, ROWS), ROWS)

    def copy(src, dst, send, recv, where):
        return pltpu.make_async_remote_copy(
            src_ref=src, dst_ref=dst, send_sem=send, recv_sem=recv, device_id=where, device_id_type=MESH
        )

    def scatter(d, src, dst, send, recv):
        there = onward(d)
        return copy(src.at[rows_of(there)], dst.at[lo], send.at[d], recv.at[d], {"lo": there, "hi": hi})

    def scatter_top(d):
        return scatter(d, pt_top, rs_top, su_s, su_r)

    def scatter_low(d):
        return scatter(d, pt_low, rs_low, sd_s, sd_r)

    def gather_top(d):
        return copy(ct_top.at[mine], ct_top.at[mine], gu_s.at[d], gu_r.at[d], {"lo": onward(d), "hi": hi})

    def gather_low(d):
        there = onward(d)
        return copy(ag_low.at[there], ct_low.at[mine], gd_s.at[d], gd_r.at[d], {"lo": there, "hi": hi})

    def near_top(m):
        return copy(q_top, a_in.at[m - 1], a_s.at[m - 1], a_r.at[m - 1], {"lo": lo, "hi": flip(hi, m)})

    def near_low(m):
        src = q_low.at[:, 0:RANK] if m == 1 else q_low.at[:, RANK : 2 * RANK]
        return copy(src, e_in.at[m - 1], e_s.at[m - 1], e_r.at[m - 1], {"lo": lo, "hi": flip(hi, m)})

    def far_top(m):
        level = 0 if m == 1 else 1 if m < 4 else 2
        src = g_top.at[:, level * RANK : (level + 1) * RANK]
        return copy(src, b_in.at[m - 1], b_s.at[m - 1], b_r.at[m - 1], {"lo": lo, "hi": flip(hi, 4 * m)})

    def each(fn):
        def step(d, c):
            fn(d)
            return c

        lax.fori_loop(1, LO, step, 0)

    barrier = pltpu.get_barrier_semaphore()
    each(lambda d: pl.semaphore_signal(barrier, inc=1, device_id={"lo": onward(d), "hi": hi}, device_id_type=MESH))
    for m in range(1, 4):
        pl.semaphore_signal(barrier, inc=1, device_id={"lo": lo, "hi": flip(hi, m)}, device_id_type=MESH)
    quad = hi // 4

    def upper(m):
        return quad // (1 << (m.bit_length() - 1)) % 2 == 1

    for m in range(1, 8):

        @pl.when(jnp.logical_not(upper(m)))
        def _():
            pl.semaphore_signal(barrier, inc=1, device_id={"lo": lo, "hi": flip(hi, 4 * m)}, device_id_type=MESH)

    rank = jnp.minimum(quad, 4) + jnp.where(x + y < 2, 0, jnp.where(quad == 3, 2, 1))
    rank = jnp.where(lo + hi == 0, 3, rank)
    places = []
    for choice in zip(*PLACES):
        place = choice[-1]
        for k in range(len(choice) - 2, -1, -1):
            place = jnp.where(rank == k, choice[k], place)
        places.append(place)

    pad = DEPTH - WIDTH - 16
    arriving[0].wait()
    for c in range(0, PTS, COLS):
        cut = slice(c, c + COLS)
        xr[0:WIDTH, cut] = points[:, cut]
        xr[WIDTH : WIDTH + 16, cut] = extended(points[:, cut].astype(f32), 0.0, 1.0, False).astype(bf16)
        xr[WIDTH + 16 : DEPTH, cut] = jnp.zeros((pad, COLS), bf16)

    sets = [2 + FIRST + j for j in range(TOP)] + [2 + j for j in range(LOW)] + [0, 1]

    def anchor_rows(first, last):
        for k in range(first, last):
            s = sets[k]
            cols = anchors[s].astype(f32)
            sign = SIGN * (2 * s - 1) if s < 2 else 0.0
            offset = -SIGN * SIGN if s < 2 else 0.0
            left = jnp.concatenate([cols, extended(cols, sign, offset, True), jnp.zeros((pad, RANK), f32)], 0)
            zlt[k * RANK : (k + 1) * RANK, :] = left.T.astype(bf16)

    arriving[1].wait()
    anchor_rows(0, TOP)
    arriving[2].wait()
    for c in range(0, PTS, COLS):
        cut = slice(c, c + COLS)
        xt[:, cut] = rhs[cut, :].T

    def basis(first, width, piece, sums):
        total = None
        for c in range(0, PTS, piece):
            cut = slice(c, c + piece)
            tile = gauss(zlt[first : first + width], xr[:, cut])
            vt[first : first + width, cut] = tile
            part = dot_nt(xt[:, cut], tile)
            total = part if total is None else total + part
        sums[...] = total

    basis(0, TOPW, 1024, pt_top)
    pl.semaphore_wait(barrier, LO - 1 + 3 + quad)
    for m in range(1, 8):

        @pl.when(upper(m))
        def _():
            pl.semaphore_signal(ready, inc=1, device_id={"lo": lo, "hi": flip(hi, 4 * m)}, device_id_type=MESH)

    for d in WAYS:
        scatter_top(d).start()
    rs_top[lo] = pt_top[mine, :]
    anchor_rows(TOP, TOP + LOW)
    basis(TOPW, LOWW, 1024, pt_low)
    def send_near():
        each(lambda d: scatter_top(d).wait_recv())
        total = rs_top[0]
        for g in range(1, LO):
            total = total + rs_top[g]
        q_top[...] = total
        for m in range(1, 4):
            near_top(m).start()

    def send_far():
        for m in range(1, 4):
            near_top(m).wait_recv()
        g_top[...] = (q_top[...] + a_in[0]) + (a_in[1] + a_in[2])
        for m in range(1, 8):
            pl.when(upper(m))(far_top(m).start)

    def send_up():
        @pl.when(quad < 7)
        def _():
            pl.semaphore_wait(ready, 7 - quad)

        for m in range(1, 8):
            pl.when(jnp.logical_not(upper(m)))(far_top(m).start)

    pl.when(places[0] == -3)(send_near)
    start_low = lambda: each(lambda d: scatter_low(d).start())
    pl.when(rank != 4)(start_low)
    rs_low[lo] = pt_low[mine, :]

    arriving[3].wait()
    lane_hot, row_hot = [], []
    for k in range(LEAF // 128, PTS // 128):
        line = order[k : k + 1, :]
        lane_hot.append(jnp.where(lax.broadcasted_iota(jnp.int32, (128, 128), 0) == (line & 127), 1.0, 0.0).astype(bf16))
        row_hot.append(jnp.where(lax.broadcasted_iota(jnp.int32, (32, 128), 0) == (line >> 7), 1.0, 0.0).astype(bf16))
    in_second = dot_nt(jnp.concatenate(row_hot, 1), jnp.concatenate(lane_hot, 1))
    signs = (2.0 * in_second - 1.0) * SIGN
    for k in range(PTS // 128):
        srow[:, k * 128 : (k + 1) * 128] = signs[k : k + 1, :]
    for c in range(0, PTS, COLS):
        cut = slice(c, c + COLS)
        cols = points[:, cut].astype(f32)
        xr[WIDTH : WIDTH + 16, cut] = extended(cols, srow[:, cut], 1.0, False).astype(bf16)
        left = jnp.concatenate([cols, extended(cols, srow[:, cut], -SIGN * SIGN, True), jnp.zeros((pad, COLS), f32)], 0)
        xlt[cut, :] = left.T.astype(bf16)
    anchor_rows(TOP + LOW, TOP + LOW + 2)

    pl.when(places[0] == -1)(send_near)
    pl.when(rank == 4)(start_low)
    pl.when(places[1] == -1)(send_far)
    basis(FARW, 2 * RANK, 2048, et)
    arriving[4].wait()

    def mix(coef, core, scale):
        return dot_nt(coef * scale, core, precision=lax.Precision.HIGHEST).astype(bf16)

    for a in range(2):
        coef = et[:, (1 - a) * RANK : (2 - a) * RANK]
        tt[:, FARW + a * RANK : FARW + (a + 1) * RANK] = mix(coef, coupling[a], 1.0 / math.sqrt(LEAF))

    def sum_low():
        each(lambda d: scatter_low(d).wait_recv())
        lanes = slice(INSIDE * RANK, LOWW)
        total = rs_low[0, :, lanes]
        for g in range(1, LO):
            total = total + rs_low[g, :, lanes]
        q_low[...] = total
        for m in range(1, 4):
            near_low(m).start()
        for j in range(INSIDE):
            lanes = slice(j * RANK, (j + 1) * RANK)
            sums = [rs_low[g, :, lanes] for g in range(LO)]
            for _ in range(j):
                sums = [sums[2 * k] + sums[2 * k + 1] for k in range(len(sums) // 2)]
            for g in range(LO):
                ag_low[g, :, lanes] = sums[(g >> j) ^ 1]

    def send_low():
        for m in range(1, 4):
            near_low(m).wait_recv()
        fourth, fifth = e_in[0], e_in[1] + e_in[2]
        for g in range(LO):
            ag_low[g, :, INSIDE * RANK : (INSIDE + 1) * RANK] = fourth
            ag_low[g, :, (INSIDE + 1) * RANK : LOWW] = fifth
        each(lambda d: gather_low(d).start())
        ct_low[mine, :] = ag_low[lo]

    def send_top():
        for m in range(1, 8):
            far_top(m).wait_recv()
        ct_top[mine, 0:RANK] = b_in[0]
        ct_top[mine, RANK : 2 * RANK] = b_in[1] + b_in[2]
        ct_top[mine, 2 * RANK : 3 * RANK] = (b_in[3] + b_in[4]) + (b_in[5] + b_in[6])
        for d in WAYS:
            gather_top(d).start()

    def dense(i, c):
        for at, what in zip(places, (send_near, send_far, send_up, sum_low, send_low, send_top)):
            pl.when(i == at)(what)
        cut = pl.ds(pl.multiple_of(i * STEP, STEP), STEP)
        right = xr[:, cut]
        total = dot(tt[:, FARW:ALLW], vt[FARW:ALLW, cut])
        for r in range(0, PTS, LEAF):
            total = total + dot(xt[:, r : r + LEAF], gauss(xlt[r : r + LEAF, :], right))
        yt[:, cut] = total
        return c

    lax.fori_loop(0, PTS // STEP, dense, 0)

    each(lambda d: gather_low(d).wait_recv())
    for j in range(LOW):
        scale = 1.0 / math.sqrt(PTS * 2.0**j)
        tt[:, TOPW + j * RANK : TOPW + (j + 1) * RANK] = mix(ct_low[:, j * RANK : (j + 1) * RANK], coupling[2 + j], scale)
    yt[...] += dot(tt[:, TOPW:FARW], vt[TOPW:FARW, :])
    each(lambda d: scatter_top(d).wait_send())
    each(lambda d: scatter_low(d).wait_send())
    each(lambda d: gather_low(d).wait_send())
    for m in range(1, 4):
        near_top(m).wait_send()
        near_low(m).wait_send()
    for m in range(1, 8):
        far_top(m).wait_send()
    each(lambda d: gather_top(d).wait_send())
    each(lambda d: gather_top(d).wait_recv())
    for j in range(TOP):
        scale = 1.0 / math.sqrt(PTS * 2.0 ** (FIRST + j))
        tt[:, j * RANK : (j + 1) * RANK] = mix(ct_top[:, j * RANK : (j + 1) * RANK], coupling[2 + FIRST + j], scale)
    out[...] = (yt[...] + dot(tt[:, 0:TOPW], vt[0:TOPW, :])).T


def per_device(points, rhs, order, anchors, coupling):
    given = (points[0, 0], rhs[0, 0], order[0, 0].reshape(PTS // 128, 128), anchors[0, 0], coupling[0, 0])
    scratch = [(a.shape, a.dtype) for a in given] + [
        ((DEPTH, PTS), bf16),
        ((PTS, DEPTH), bf16),
        ((ALLW, DEPTH), bf16),
        ((RHS, PTS), bf16),
        ((ALLW, PTS), bf16),
        ((RHS, PTS), f32),
        ((RHS, ALLW), bf16),
        ((1, PTS), f32),
        ((RHS, TOPW), f32),
        ((RHS, LOWW), f32),
        ((RHS, 2 * RANK), f32),
        ((LO, ROWS, TOPW), f32),
        ((LO, ROWS, LOWW), f32),
        ((ROWS, TOPW), f32),
        ((ROWS, 2 * RANK), f32),
        ((3, ROWS, TOPW), f32),
        ((3, ROWS, RANK), f32),
        ((ROWS, TOPW), f32),
        ((7, ROWS, RANK), f32),
        ((RHS, TOPW), f32),
        ((RHS, LOWW), f32),
        ((LO, ROWS, LOWW), f32),
    ]
    sems = [pltpu.SemaphoreType.DMA((n,)) for n in [5] + [LO] * 8 + [3] * 4 + [7] * 2]
    sems.append(pltpu.SemaphoreType.REGULAR)
    out = pl.pallas_call(
        body,
        out_shape=pltpu.VMEM((PTS, RHS), f32),
        in_specs=[pl.BlockSpec(memory_space=pltpu.HBM)] * 5,
        out_specs=pl.BlockSpec(memory_space=pltpu.VMEM),
        scratch_shapes=[pltpu.VMEM(s, d) for s, d in scratch] + sems,
        compiler_params=pltpu.CompilerParams(
            collective_id=0, has_side_effects=True, vmem_limit_bytes=60 * 2**20
        ),
        name="hodlr",
    )(*given)
    return out[None, None]


def solution(mesh):
    return jax.shard_map(
        per_device,
        mesh=mesh,
        in_specs=(
            P("hi", "lo", None, None),
            P("hi", "lo", None, None),
            P("hi", "lo", None),
            P("hi", "lo", None, None, None),
            P("hi", "lo", None, None, None),
        ),
        out_specs=P("hi", "lo", None, None),
        check_vma=False,
    )
```
